512 devices in a mesh: dp: 64 (over z, y), mp: 8 (over x, core).
Axes of the slice: x: 4, y: 8, z: 8, core: 2. Of those that a mesh axis runs over, the one named last changes fastest.
Arguments:
- gradients: float32 [64, 4, 128, 8192], P('dp', None, 'mp'), may hold values from -16 to 16
- weights: float32 [4, 128, 8192], P(None, 'mp', 'dp'), may hold values from -40 to 40
- first_moment: float32 [4, 128, 8192], P(None, 'mp', 'dp'), may hold values from -0.6 to 0.6
- second_moment: float32 [4, 128, 8192], P(None, 'mp', 'dp'), may hold values from 0.001 to 0.1
- learn_rate: float32 [4], replicated, may hold values from 0.1 to 0.5
- weight_decay: float32 [4], replicated, may hold values from 0.1 to 1
Outputs:
- new_weights: float32 [4, 128, 8192], P(None, 'mp')
- new_first: float32 [4, 128, 8192], P(None, 'mp', 'dp')
- new_second: float32 [4, 128, 8192], P(None, 'mp', 'dp')
- trust_ratio: float32 [4], replicated
The draws below stay inside these ranges and needn't reach their ends.
All inputs are finite; a program needn't handle non-finite values.
Results may differ from the reference program's by a relative error of at most 0.000062.
Values sent between devices are 32-bit elements; how exact they have to be, the bound alone decides.
A program may use at most 64 MiB of HBM per device.

```python
import math
import jax
import jax.numpy as jnp
from jax import lax

D = 8192
NT = 4
STEP = 10
ROWS = 128
REPLICAS = 64
N_DP = 64


def draw_weights(key, part):
    base_key = jax.random.fold_in(key, 11)
    row_key = jax.random.fold_in(key, 12)
    col_key = jax.random.fold_in(key, 13)
    row_place = jnp.arange(ROWS, dtype=jnp.float32) / ROWS
    col_place = jnp.arange(D, dtype=jnp.float32) / D
    row_scale = jnp.exp(math.log(3.0) * row_place + jax.random.uniform(row_key, (ROWS,), jnp.float32, 0.0, math.log(3.3)))
    col_scale = jnp.exp(math.log(3.0) * col_place + jax.random.uniform(col_key, (D,), jnp.float32, 0.0, math.log(3.3)))
    base = jax.random.truncated_normal(base_key, -4.0, 4.0, (NT, ROWS, D), jnp.float32)
    return 0.1 * base * row_scale[None, :, None] * col_scale[None, None, :]


def spiked(array, key, source, target, shards_of, factor):
    def block_of(position):
        return (jnp.arange(array.shape[position]) // (array.shape[position] // shards_of)).reshape((-1,) + (1,) * (array.ndim - 1 - position))

    one_side = jax.random.permutation(key, shards_of)[block_of(target)]
    far = (block_of(target) + shards_of // 2) % shards_of
    return jnp.where((block_of(source) == one_side) | (block_of(source) == far), factor * array, array)


def block_levels(rng, dims, cuts, least, top_value):
    gain = 1.0
    for position, shards_of in cuts:
        draws = jax.random.uniform(jax.random.fold_in(jax.random.fold_in(rng, 6), position), (shards_of,), jnp.float32, least / len(cuts), top_value / len(cuts))
        gain = gain * jnp.repeat(jnp.exp(draws), dims[position] // shards_of).reshape((-1,) + (1,) * (len(dims) - 1 - position))
    return gain


def centred(rng, extent, width, bound, split=(), held_as=jnp.bfloat16):
    drawn = width * jax.random.normal(rng, extent, jnp.float32)
    if split:
        drawn = drawn * block_levels(rng, extent, split, -0.22, 0.18)
    return jnp.clip(drawn, -bound, bound).astype(held_as)


def heavy_noise(key, shape, scale, bound, cuts, heavy, kind=jnp.bfloat16):
    result = scale * jax.random.normal(key, shape, jnp.float32)
    if cuts:
        result = result * block_levels(key, shape, cuts, -0.22, 0.18)
    return jnp.clip(spiked(result, jax.random.fold_in(key, 3), *heavy), -bound, bound).astype(kind)


def setup_inputs(seed: int = 0) -> dict:
    key_list = jax.random.split(jax.random.key(seed), 7)
    gradients = heavy_noise(key_list[0], (REPLICAS, NT, ROWS, D), 1.0, 16.0, ((0, 64), (2, 8)), (0, 3, 64, 4.0), jnp.float32)
    weights = draw_weights(jax.random.fold_in(key_list[6], 71), 0)
    first_moment = centred(key_list[2], (NT, ROWS, D), 0.1, 0.6, ((1, 8), (2, 64)), jnp.float32)
    second_moment = jnp.clip(jnp.exp(math.log(0.1) - 4.6051702 * jax.random.uniform(key_list[3], (NT, ROWS, D), jnp.float32) ** block_levels(key_list[3], (NT, ROWS, D), ((1, 8), (2, 64)), -0.2, 0.2)), 0.001, 0.1)
    learn_rate = jnp.clip(jnp.exp(jax.random.uniform(key_list[4], (NT,), jnp.float32, math.log(0.1), math.log(0.5))), 0.1, 0.5)
    weight_decay = jnp.clip(jax.random.uniform(key_list[5], (NT,), jnp.float32, 0.1, 1.0), 0.1, 1.0)
    return {"gradients": gradients, "weights": weights, "first_moment": first_moment, "second_moment": second_moment, "learn_rate": learn_rate, "weight_decay": weight_decay}


def reference(gradients, weights, first_moment, second_moment, learn_rate, weight_decay):
    summed = lax.optimization_barrier(jnp.sum(gradients, axis=0)) * (1.0 / N_DP)
    new_first = 0.9 * first_moment + 0.1 * summed
    new_second = 0.999 * second_moment + 0.001 * summed * summed
    first_fix = 1.0 - 0.9 ** STEP
    second_fix = 1.0 - 0.999 ** STEP
    update = new_first / first_fix / (jnp.sqrt(new_second / second_fix) + 1e-06) + weight_decay[:, None, None] * weights
    weight_sq = lax.optimization_barrier(jnp.sum(weights * weights, axis=(1, 2)))
    update_sq = lax.optimization_barrier(jnp.sum(update * update, axis=(1, 2)))
    trust_ratio = jnp.sqrt(weight_sq) / (jnp.sqrt(update_sq) + 1e-06)
    new_weights = weights - (learn_rate * trust_ratio)[:, None, None] * update
    return (new_weights, new_first, new_second, trust_ratio)
```

```python
import functools

import jax
import jax.numpy as jnp
from jax import lax
from jax.experimental import pallas as pl
from jax.experimental.pallas import tpu as pltpu
from jax.sharding import PartitionSpec as P

STEP = 10
NT = 4
SIDE = 8
F32 = jnp.float32
MESH = pl.DeviceIdType.MESH

LATE = (0, 1, 2, 3)


def order():
    steps = []
    for s in range(1, 5):
        steps += [("reduce", t, s) for t in range(NT)]
        steps += [("near_weights", s)]
    for t in range(NT):
        steps += [("spread", t)]
    steps += [("near_weights", 5)]
    for t in range(NT):
        steps += [("update", t)]
    for t in range(NT):
        steps += [("squares", t)]
    steps += [("total", 0), ("total", 1), ("total", 2)]
    for s in range(1, 5):
        steps += [("late", t, s) for t in range(NT)]
    for t in range(NT):
        steps += [("finish", t)]
    return steps


def length(t, h, d):
    return 4 if (t + h + d) % 2 == 0 else 3


def kernel(
    g_hbm, w_hbm, m_hbm, v_hbm, lr, wd,
    out_hbm, nf_hbm, ns_hbm, tr_out,
    g, w, m, v, nf, ns, ring, own, cross, u1, w1, out, sq_a, sq_b, sq_m, squares,
    load_g, load_s, ring_s, ring_r, cross_s, cross_r, u1_s, u1_r, w1_s, w1_r, sq_s, sq_r, ag_s, ag_r, out_s,
):
    dp, mp = lax.axis_index("dp"), lax.axis_index("mp")
    z, y = dp // SIDE, dp % SIDE

    def mod(i):
        return lax.rem(i + 2 * SIDE, SIDE)

    def ring_peer(h, k):
        return (z * SIDE + mod(y + k), mp) if h == 0 else (mod(z + k) * SIDE + y, mp)

    def cross_peer(h, k):
        return ring_peer(1 - h, k)

    def ring_at(h):
        return y if h == 0 else z

    def cross_at(h):
        return z if h == 0 else y

    def chunk(ref, t, h, r):
        return ref.at[t, 0, :, r] if h == 0 else ref.at[t, 1, r]

    def tile(ref, t, h, r, c):
        return ref.at[t, 0, c, r] if h == 0 else ref.at[t, 1, r, c]

    def send(src, dst, ss, rs, to):
        copy = pltpu.make_async_remote_copy(
            src_ref=src, dst_ref=dst, send_sem=ss, recv_sem=rs, device_id=to, device_id_type=MESH
        )
        copy.start()

    def arrived(ref, sem):
        pltpu.make_async_copy(ref, ref, sem).wait()

    loads = []
    for t in range(NT):
        for h in range(2):
            loads.append(pltpu.make_async_copy(g_hbm.at[t, h], g.at[t, h], load_g.at[t, h]))
    small = [
        pltpu.make_async_copy(a, b, load_s.at[i])
        for i, (a, b) in enumerate(((w_hbm, w), (m_hbm, m), (v_hbm, v)))
    ]
    for c in loads + small:
        c.start()

    barrier = pltpu.get_barrier_semaphore()
    near = [ring_peer(h, k) for h in range(2) for k in (1, -1)] + [(dp, mod(mp + k)) for k in range(1, SIDE)]
    for peer in near:
        pl.semaphore_signal(barrier, inc=1, device_id=peer, device_id_type=MESH)
    pl.semaphore_wait(barrier, len(near))

    first_fix = 1.0 - 0.9**STEP
    second_fix = 1.0 - 0.999**STEP
    scale = {}

    def reduce(t, s):
        for h in range(2):
            if s == 1:
                loads[2 * t + h].wait()
            for d, sign in enumerate((1, -1)):
                n = length(t, h, d)
                if s > n:
                    continue
                mine = chunk(g, t, h, mod(ring_at(h) + sign * (n - s + 1)))
                if s == 1:
                    src = mine
                else:
                    src = ring.at[t, h, d, s - 2]
                    arrived(src, ring_r.at[t, h, d, s - 2])
                    src[...] += mine[...]
                send(src, ring.at[t, h, d, s - 1], ring_s, ring_r.at[t, h, d, s - 1], ring_peer(h, sign))

    def near_weights(s):
        if s == 1:
            for c in small:
                c.wait()
            for h in range(2):
                w1[h, cross_at(h)] = w[:, h]
        for h in range(2):
            for d, sign in enumerate((1, -1)):
                n = length(0, h, d)
                if 1 < s <= n + 1:
                    at = w1.at[h, mod(cross_at(h) - sign * (s - 1))]
                    arrived(at, w1_r.at[h, d, s - 2])
                if s <= n:
                    at = w1.at[h, mod(cross_at(h) - sign * (s - 1))]
                    send(at, at, w1_s, w1_r.at[h, d, s - 1], cross_peer(h, sign))

    def spread(t):
        for h in range(2):
            total = chunk(g, t, h, ring_at(h))[...]
            for d in range(2):
                last = length(t, h, d) - 1
                arrived(ring.at[t, h, d, last], ring_r.at[t, h, d, last])
                total += ring[t, h, d, last]
            own[t, h] = total
        for h in range(2):
            for k in (4, 3, 5, 2, 6, 1, 7):
                send(
                    own.at[t, h, mod(cross_at(h) + k)], cross.at[t, h, cross_at(h)],
                    cross_s, cross_r.at[t, h], cross_peer(h, k),
                )

    def update(t):
        for h in range(2):
            cross[t, h, cross_at(h)] = own[t, h, cross_at(h)]
            arrived(cross.at[t, h, 0:7], cross_r.at[t, h])
            summed = jnp.sum(cross[t, h], axis=0) * (1.0 / (SIDE * SIDE))
            new_first = 0.9 * m[t, h] + 0.1 * summed
            new_second = 0.999 * v[t, h] + 0.001 * summed * summed
            nf[t, h] = new_first
            ns[t, h] = new_second
            u1[t, h, cross_at(h)] = (
                new_first / first_fix / (jnp.sqrt(new_second / second_fix) + 1e-06) + wd[t] * w[t, h]
            )
            at = u1.at[t, h, cross_at(h)]
            for k in (4, 3, 5, 2, 6, 1, 7):
                send(at, at, u1_s, u1_r.at[t, h], cross_peer(h, k))

    def squared(a):
        return jnp.sum(jnp.sum(a * a, axis=0), axis=0, keepdims=True)

    def squares_of(t):
        for h in range(2):
            arrived(u1.at[t, h, 0:7], u1_r.at[t, h])
            squares[h, t : t + 1] = squared(w1[h, :, t])
            squares[h, NT + t : NT + t + 1] = squared(u1[t, h])

    def total(stage):
        if stage == 0:
            for h, slots in enumerate((sq_a, sq_b)):
                slots[ring_at(h)] = squares[h]
                for k in (4, 3, 5, 2, 6, 1, 7):
                    send(squares.at[h], slots.at[ring_at(h)], sq_s, sq_r.at[h], ring_peer(h, k))
        if stage == 1:
            for h, slots in enumerate((sq_a, sq_b)):
                arrived(slots.at[0:7], sq_r.at[h])
            squares[2] = jnp.sum(sq_a[...], axis=0) + jnp.sum(sq_b[...], axis=0)
            sq_m[mp] = squares[2]
            for k in (4, 3, 5, 2, 6, 1, 7):
                send(squares.at[2], sq_m.at[mp], sq_s, sq_r.at[2], (dp, mod(mp + k)))
        if stage == 2:
            arrived(sq_m.at[0:7], sq_r.at[2])
            both = jnp.sum(sq_m[...], axis=0)
            for t in range(NT):
                weight_sq = jnp.sum(both[t : t + 1], axis=1, keepdims=True)
                update_sq = jnp.sum(both[NT + t : NT + t + 1], axis=1, keepdims=True)
                ratio = jnp.sqrt(weight_sq) / (jnp.sqrt(update_sq) + 1e-06)
                tr_out[t] = jnp.max(ratio)
                scale[t] = lr[t] * ratio

    def around(ref, t, s, sems, sem):
        for h in range(2):
            for d, sign in enumerate((1, -1)):
                n = length(t, h, d)
                at = chunk(ref, t, h, mod(ring_at(h) - sign * (s - 1)))
                if 1 < s <= n + 1:
                    arrived(at, sems.at[t, h, d, s - 2])
                if s <= n:
                    send(at, at, sem, sems.at[t, h, d, s - 1], ring_peer(h, sign))

    def late(t, s):
        if s == 1:
            for h in range(2):
                chunk(out, t, h, ring_at(h))[...] = w1[h, :, t] - scale[t][None] * u1[t, h]
        around(out, t, s, ag_r, ag_s)

    def finish(t):
        around(out, t, 5, ag_r, ag_s)
        pltpu.make_async_copy(out.at[t], out_hbm.at[t], out_s.at[t]).start()

    acts = {
        "reduce": reduce, "near_weights": near_weights, "spread": spread, "update": update,
        "squares": squares_of, "total": total, "late": late, "finish": finish,
    }
    for name, *args in order():
        acts[name](*args)
        if name == "update" and args[0] == NT - 1:
            outs = [
                pltpu.make_async_copy(nf, nf_hbm, out_s.at[NT]),
                pltpu.make_async_copy(ns, ns_hbm, out_s.at[NT + 1]),
            ]
            for c in outs:
                c.start()

    arrived(g.at[:, :, 0:7], ring_s)
    arrived(g.at[:, :, 0:7], ag_s)
    arrived(g.at[0, 0, 0:7], cross_s)
    arrived(g.at[0, 0, 0:7], u1_s)
    arrived(g.at[0, 0, 0:7], w1_s)
    arrived(g.at[0, 0:1, 0:3, 0:7], sq_s)
    for t in range(NT):
        pltpu.make_async_copy(out.at[t], out_hbm.at[t], out_s.at[t]).wait()
    for c in outs:
        c.wait()


def shards(gradients, weights, first_moment, second_moment, learn_rate, weight_decay):
    tiles = (NT, 2, SIDE, SIDE, 8, 128)
    mine = (NT, 2, 8, 128)
    g = gradients.reshape(NT, 2, 8, SIDE, SIDE, 128).transpose(0, 1, 3, 4, 2, 5)
    dma = pltpu.SemaphoreType.DMA
    any_space = pl.BlockSpec(memory_space=pl.ANY)
    smem = pl.BlockSpec(memory_space=pltpu.SMEM)
    out, nf, ns, tr = pl.pallas_call(
        kernel,
        out_shape=(
            jax.ShapeDtypeStruct(tiles, F32),
            jax.ShapeDtypeStruct(mine, F32),
            jax.ShapeDtypeStruct(mine, F32),
            jax.ShapeDtypeStruct((NT,), F32),
        ),
        in_specs=[any_space] * 4 + [smem] * 2,
        out_specs=(any_space, any_space, any_space, smem),
        scratch_shapes=[
            pltpu.VMEM(tiles, F32),
            *[pltpu.VMEM(mine, F32)] * 5,
            pltpu.VMEM((NT, 2, 2, 4, SIDE, 8, 128), F32),
            pltpu.VMEM((NT, 2, SIDE, 8, 128), F32),
            pltpu.VMEM((NT, 2, SIDE, 8, 128), F32),
            pltpu.VMEM((NT, 2, SIDE, 8, 128), F32),
            pltpu.VMEM((2, SIDE, NT, 8, 128), F32),
            pltpu.VMEM(tiles, F32),
            *[pltpu.VMEM((SIDE, 8, 128), F32)] * 3,
            pltpu.VMEM((3, 8, 128), F32),
            dma((NT, 2)), dma((3,)),
            dma, dma((NT, 2, 2, 4)),
            dma, dma((NT, 2)),
            dma, dma((NT, 2)),
            dma, dma((2, 2, 4)),
            dma, dma((3,)),
            dma, dma((NT, 2, 2, 4)),
            dma((NT + 2,)),
        ],
        compiler_params=pltpu.CompilerParams(
            collective_id=0, has_side_effects=True, vmem_limit_bytes=48 * 2**20
        ),
        name="lamb",
    )(
        g, *(a.reshape(mine) for a in (weights, first_moment, second_moment)), learn_rate, weight_decay
    )
    new_weights = out.transpose(0, 1, 4, 2, 3, 5).reshape(NT, 16, SIDE * SIDE * 128)
    return new_weights, nf.reshape(NT, 16, 128), ns.reshape(NT, 16, 128), tr


def solution(mesh):
    in_specs = (
        P("dp", None, "mp", None),
        P(None, "mp", "dp"),
        P(None, "mp", "dp"),
        P(None, "mp", "dp"),
        P(),
        P(),
    )
    out_specs = (P(None, "mp", None), P(None, "mp", "dp"), P(None, "mp", "dp"), P())
    return jax.shard_map(shards, mesh=mesh, in_specs=in_specs, out_specs=out_specs, check_vma=False)
```

```python
import functools

import jax
import jax.numpy as jnp
from jax import lax
from jax.experimental import pallas as pl
from jax.experimental.pallas import tpu as pltpu
from jax.sharding import PartitionSpec as P

STEP = 10
NT = 4
SIDE = 8
F32 = jnp.float32
MESH = pl.DeviceIdType.MESH


def order():
    every = range(NT)
    steps = [("near_weights", 1)]
    for s in range(1, 5):
        steps += [("reduce", t, s) for t in every] + [("near_weights", s + 1)] * (s < 4)
    steps += [("spread", t) for t in every] + [("near_weights", 5)]
    steps += [("weights", t, 1) for t in every]
    steps += [("update", t) for t in every]
    steps += [("weights", t, 2) for t in every]
    for t in every:
        steps += [("near_updates", t), ("updates", t, 1)]
    steps += [("squares", t) for t in every] + [("total", 0)]
    steps += [("updates", t, 2) for t in every]
    steps += [("weights", t, 3) for t in every] + [("total", 1)]
    steps += [("updates", t, 3) for t in every]
    steps += [("weights", t, 4) for t in every] + [("total", 2)]
    steps += [("updates", t, 4) for t in every]
    return steps + [("last", t) for t in every]


TO_OWNER = ((1, 4, 3), (1, -3, -2), (2, 3, 2), (2, -2, -1), (3, 2, 1), (3, -1, 0), (4, 1, 0))
FROM_OWNER = ((1, 0, 1), (1, 0, -1), (2, 1, 2), (2, -1, -2), (3, 2, 3), (3, -2, -3), (4, 3, 4))


def side(t, h):
    return 1 if (t + h) % 2 == 0 else -1


def length(t, h, d):
    return 4 if (t + h + d) % 2 == 0 else 3


def kernel(
    g_hbm, w_hbm, m_hbm, v_hbm, lr_hbm, wd_hbm,
    all_w, all_u, scale_out, nf_out, ns_out, tr_out,
    g, w, m, v, nf, ns, lr, wd, ring, own, cross, u1, w1, w_own, scale, sq_a, sq_b, sq_m, squares,
    load_g, load_s, ring_s, ring_r, cross_s, cross_r, u1_s, u1_r, w1_s, w1_r, sq_s, sq_r, aw_s, aw_r, au_s, au_r, out_s, res_s,
):
    dp, mp = lax.axis_index("dp"), lax.axis_index("mp")
    z, y = dp // SIDE, dp % SIDE

    def mod(i):
        return lax.rem(i + 2 * SIDE, SIDE)

    def ring_peer(h, k):
        return (z * SIDE + mod(y + k), mp) if h == 0 else (mod(z + k) * SIDE + y, mp)

    def cross_peer(h, k):
        return ring_peer(1 - h, k)

    def ring_at(h):
        return y if h == 0 else z

    def cross_at(h):
        return z if h == 0 else y

    def chunk(ref, t, h, r):
        return ref.at[t, 0, :, r] if h == 0 else ref.at[t, 1, r]

    def tile(ref, t, h, r, c):
        return ref.at[t, 0, c, r] if h == 0 else ref.at[t, 1, r, c]

    def send(src, dst, ss, rs, to):
        copy = pltpu.make_async_remote_copy(
            src_ref=src, dst_ref=dst, send_sem=ss, recv_sem=rs, device_id=to, device_id_type=MESH
        )
        copy.start()

    def arrived(ref, sem):
        pltpu.make_async_copy(ref, ref, sem).wait()

    loads = []
    for t in range(NT):
        for h in range(2):
            loads.append(pltpu.make_async_copy(g_hbm.at[t, h], g.at[t, h], load_g.at[t, h]))
    small = [
        pltpu.make_async_copy(a, b, load_s.at[i])
        for i, (a, b) in enumerate(((w_hbm, w), (m_hbm, m), (v_hbm, v), (lr_hbm, lr), (wd_hbm, wd)))
    ]
    for c in loads + small:
        c.start()

    barrier = pltpu.get_barrier_semaphore()
    near = [ring_peer(h, k) for h in range(2) for k in (1, -1)] + [(dp, mod(mp + k)) for k in range(1, SIDE)]
    for peer in near:
        pl.semaphore_signal(barrier, inc=1, device_id=peer, device_id_type=MESH)
    pl.semaphore_wait(barrier, len(near))

    first_fix = 1.0 - 0.9**STEP
    second_fix = 1.0 - 0.999**STEP
    held, seen = [], set()

    def keep(src, dst, sem):
        held.append(pltpu.make_async_copy(src, dst, sem))
        held[-1].start()

    def block_sum(t, h, at):
        mine = chunk(g, t, h, mod(ring_at(h) - side(t, h) * at))
        parts = [ring.at[t, h, a % SIDE] for _, a, b in TO_OWNER if b == at]
        for _, a, b in TO_OWNER:
            if b == at:
                arrived(ring.at[t, h, a % SIDE], ring_r.at[t, h, a % SIDE])
        return mine, parts

    def reduce(t, s):
        for h in range(2):
            if s == 1:
                loads[2 * t + h].wait()
            for step, a, b in TO_OWNER:
                if step == s:
                    src, parts = block_sum(t, h, a)
                    if parts:
                        total = src[...]
                        for part in parts:
                            total += part[...]
                        src = parts[0]
                        src[...] = total
                    send(
                        src, ring.at[t, h, a % SIDE], ring_s, ring_r.at[t, h, a % SIDE],
                        ring_peer(h, side(t, h) * (b - a)),
                    )

    def near_weights(s):
        if s == 1:
            for c in small:
                c.wait()
            for h in range(2):
                w1[h, cross_at(h)] = w[:, h]
        for h in range(2):
            for d, sign in enumerate((1, -1)):
                n = length(0, h, d)
                if 1 < s <= n + 1:
                    at = w1.at[h, mod(cross_at(h) - sign * (s - 1))]
                    arrived(at, w1_r.at[h, d, s - 2])
                if s <= n:
                    at = w1.at[h, mod(cross_at(h) - sign * (s - 1))]
                    send(at, at, w1_s, w1_r.at[h, d, s - 1], cross_peer(h, sign))

    def spread(t):
        for h in range(2):
            src, parts = block_sum(t, h, 0)
            total = src[...]
            for part in parts:
                total += part[...]
            own[t, h] = total
        for h in range(2):
            for k in (4, 3, 5, 2, 6, 1, 7):
                send(
                    own.at[t, h, mod(cross_at(h) + k)], cross.at[t, h, cross_at(h)],
                    cross_s, cross_r.at[t, h], cross_peer(h, k),
                )

    def update(t):
        for h in range(2):
            cross[t, h, cross_at(h)] = own[t, h, cross_at(h)]
            arrived(cross.at[t, h, 0:7], cross_r.at[t, h])
            summed = jnp.sum(cross[t, h], axis=0) * (1.0 / (SIDE * SIDE))
            new_first = 0.9 * m[t, h] + 0.1 * summed
            new_second = 0.999 * v[t, h] + 0.001 * summed * summed
            nf[t, h] = new_first
            ns[t, h] = new_second
            u1[t, h, cross_at(h)] = (
                new_first / first_fix / (jnp.sqrt(new_second / second_fix) + 1e-06) + wd[t] * w[t, h]
            )
            at = u1.at[t, h, cross_at(h)]
            for k in (4, 3, 5, 2, 6, 1, 7):
                send(at, at, u1_s, u1_r.at[t, h], cross_peer(h, k))

    def squared(a):
        return jnp.sum(jnp.sum(a * a, axis=0), axis=0, keepdims=True)

    def near_updates(t):
        for h in range(2):
            arrived(u1.at[t, h, 0:7], u1_r.at[t, h])

    def squares_of(t):
        for h in range(2):
            squares[h, t : t + 1] = squared(w1[h, :, t])
            squares[h, NT + t : NT + t + 1] = squared(u1[t, h])

    def total(stage):
        if stage == 0:
            for h, slots in enumerate((sq_a, sq_b)):
                slots[ring_at(h)] = squares[h]
                for k in (4, 3, 5, 2, 6, 1, 7):
                    send(squares.at[h], slots.at[ring_at(h)], sq_s, sq_r.at[h], ring_peer(h, k))
        if stage == 1:
            for h, slots in enumerate((sq_a, sq_b)):
                arrived(slots.at[0:7], sq_r.at[h])
            squares[2] = jnp.sum(sq_a[...], axis=0) + jnp.sum(sq_b[...], axis=0)
            sq_m[mp] = squares[2]
            for k in (4, 3, 5, 2, 6, 1, 7):
                send(squares.at[2], sq_m.at[mp], sq_s, sq_r.at[2], (dp, mod(mp + k)))
        if stage == 2:
            arrived(sq_m.at[0:7], sq_r.at[2])
            both = jnp.sum(sq_m[...], axis=0)
            for t in range(NT):
                weight_sq = jnp.sum(both[t : t + 1], axis=1, keepdims=True)
                update_sq = jnp.sum(both[NT + t : NT + t + 1], axis=1, keepdims=True)
                ratio = jnp.sqrt(weight_sq) / (jnp.sqrt(update_sq) + 1e-06)
                tr_out[t] = jnp.max(ratio)
                scale[t : t + 1] = jnp.broadcast_to(lr[t] * ratio, (1, 128))
            keep(scale, scale_out, res_s.at[2])

    def around(first, ref, t, s, sems, sem):
        for h in range(2):
            for step, a, b in FROM_OWNER:
                if step == s:
                    at = chunk(ref, t, h, mod(ring_at(h) - side(t, h) * a))
                    if a:
                        landed(ref, t, h, a, sems)
                    send(
                        at if a else first.at[t, h], at, sem, sems.at[t, h, b % SIDE],
                        ring_peer(h, side(t, h) * (b - a)),
                    )

    def landed(ref, t, h, a, sems):
        if (ref is all_w, t, h, a) not in seen:
            seen.add((ref is all_w, t, h, a))
            arrived(chunk(ref, t, h, mod(ring_at(h) - side(t, h) * a)), sems.at[t, h, a % SIDE])

    def last(t):
        for h in range(2):
            for a in (1, -1, 2, -2, 3, -3, 4):
                landed(all_w, t, h, a, aw_r)
                landed(all_u, t, h, a, au_r)

    def weights(t, s):
        if s == 1:
            for h in range(2):
                w_own[t, h] = w1[h, :, t]
                keep(w_own.at[t, h], chunk(all_w, t, h, ring_at(h)), out_s.at[0, t, h])
        around(w_own, all_w, t, s, aw_r, aw_s)

    def updates(t, s):
        around(u1, all_u, t, s, au_r, au_s)
        if s == 1:
            for h in range(2):
                keep(u1.at[t, h], chunk(all_u, t, h, ring_at(h)), out_s.at[1, t, h])

    acts = {
        "reduce": reduce, "near_weights": near_weights, "spread": spread, "update": update,
        "near_updates": near_updates, "squares": squares_of, "total": total, "weights": weights, "updates": updates, "last": last,
    }
    for name, *args in order():
        acts[name](*args)
        if name == "update" and args[0] == NT - 1:
            keep(nf, nf_out, res_s.at[0])
            keep(ns, ns_out, res_s.at[1])

    arrived(g.at[:, :, 0:7], ring_s)
    arrived(g.at[:, :, 0:7], aw_s)
    arrived(g.at[:, :, 0:7], au_s)
    arrived(g.at[0, 0, 0:7], cross_s)
    arrived(g.at[0, 0, 0:7], u1_s)
    arrived(g.at[0, 0, 0:7], w1_s)
    arrived(g.at[0, 0:1, 0:3, 0:7], sq_s)
    for c in held:
        c.wait()


def results(all_w, all_u, scale, nf, ns, tr, new_out, nf_out, ns_out, tr_out, new, sem, sem_new):
    copies = [
        pltpu.make_async_copy(a, b, sem.at[i])
        for i, (a, b) in enumerate(((nf, nf_out), (ns, ns_out), (tr, tr_out)))
    ]
    for c in copies:
        c.start()
    for t in range(NT):
        for h in range(2):
            new[t, h] = all_w[t, h] - scale[t : t + 1] * all_u[t, h]
            copies.append(pltpu.make_async_copy(new.at[t, h], new_out.at[t, h], sem_new.at[t, h]))
            copies[-1].start()
    for c in copies:
        c.wait()


def shards(gradients, weights, first_moment, second_moment, learn_rate, weight_decay):
    tiles = (NT, 2, SIDE, SIDE, 8, 128)
    mine = (NT, 2, 8, 128)
    g = gradients.reshape(NT, 2, 8, SIDE, SIDE, 128).transpose(0, 1, 3, 4, 2, 5)
    dma = pltpu.SemaphoreType.DMA
    any_space = pl.BlockSpec(memory_space=pl.ANY)
    smem = pl.BlockSpec(memory_space=pltpu.SMEM)
    arrays = pl.pallas_call(
        kernel,
        out_shape=(
            jax.ShapeDtypeStruct(tiles, F32),
            jax.ShapeDtypeStruct(tiles, F32),
            jax.ShapeDtypeStruct((8, 128), F32),
            jax.ShapeDtypeStruct(mine, F32),
            jax.ShapeDtypeStruct(mine, F32),
            jax.ShapeDtypeStruct((NT,), F32),
        ),
        in_specs=[any_space] * 6,
        out_specs=(*[any_space] * 5, smem),
        scratch_shapes=[
            pltpu.VMEM(tiles, F32),
            *[pltpu.VMEM(mine, F32)] * 5,
            *[pltpu.SMEM((NT,), F32)] * 2,
            pltpu.VMEM((NT, 2, SIDE, SIDE, 8, 128), F32),
            pltpu.VMEM((NT, 2, SIDE, 8, 128), F32),
            pltpu.VMEM((NT, 2, SIDE, 8, 128), F32),
            pltpu.VMEM((NT, 2, SIDE, 8, 128), F32),
            pltpu.VMEM((2, SIDE, NT, 8, 128), F32),
            pltpu.VMEM((NT, 2, SIDE, 8, 128), F32),
            pltpu.VMEM((8, 128), F32),
            *[pltpu.VMEM((SIDE, 8, 128), F32)] * 3,
            pltpu.VMEM((3, 8, 128), F32),
            dma((NT, 2)), dma((5,)),
            dma, dma((NT, 2, SIDE)),
            dma, dma((NT, 2)),
            dma, dma((NT, 2)),
            dma, dma((2, 2, 4)),
            dma, dma((3,)),
            dma, dma((NT, 2, SIDE)),
            dma, dma((NT, 2, SIDE)),
            dma((2, NT, 2)), dma((3,)),
        ],
        compiler_params=pltpu.CompilerParams(
            collective_id=0, has_side_effects=True, vmem_limit_bytes=24 * 2**20
        ),
        name="lamb",
    )(
        *(
            pltpu.with_memory_space_constraint(a, pltpu.HBM)
            for a in (
                g, *(a.reshape(mine) for a in (weights, first_moment, second_moment)), learn_rate, weight_decay
            )
        )
    )
    vmem = pl.BlockSpec(memory_space=pltpu.VMEM)
    out, nf, ns, tr = pl.pallas_call(
        results,
        out_shape=tuple(jax.ShapeDtypeStruct(a.shape, F32) for a in (arrays[0], *arrays[3:])),
        in_specs=[vmem] * 3 + [any_space] * 3,
        out_specs=(any_space,) * 4,
        scratch_shapes=[pltpu.VMEM(tiles, F32), dma((3,)), dma((NT, 2))],
        compiler_params=pltpu.CompilerParams(vmem_limit_bytes=8 * 2**20),
        name="results",
    )(*(pltpu.with_memory_space_constraint(a, pltpu.VMEM) for a in arrays))
    new_weights = out.transpose(0, 1, 4, 2, 3, 5).reshape(NT, 16, SIDE * SIDE * 128)
    return new_weights, nf.reshape(NT, 16, 128), ns.reshape(NT, 16, 128), tr


def solution(mesh):
    in_specs = (
        P("dp", None, "mp", None),
        P(None, "mp", "dp"),
        P(None, "mp", "dp"),
        P(None, "mp", "dp"),
        P(),
        P(),
    )
    out_specs = (P(None, "mp", None), P(None, "mp", "dp"), P(None, "mp", "dp"), P())
    return jax.shard_map(shards, mesh=mesh, in_specs=in_specs, out_specs=out_specs, check_vma=False)
```

```python
import functools

import jax
import jax.numpy as jnp
from jax import lax
from jax.experimental import pallas as pl
from jax.experimental.pallas import tpu as pltpu
from jax.sharding import PartitionSpec as P

STEP = 10
GROUPS = ((0, 1), (1, 2), (2, 3), (3, 4))
FAR_FIRST = (4, 3, 5, 2, 6, 1, 7)
NT = 4
SIDE = 8
F32 = jnp.float32
MESH = pl.DeviceIdType.MESH


TO_RING = ((1, 4, 3), (1, -3, -2), (2, 3, 2), (2, -2, -1), (3, 2, 1), (3, -1, 0), (4, 1, 0))
FROM_RING = ((1, 0, 1), (1, 0, -1), (2, 1, 2), (2, -1, -2), (3, 2, 3), (3, -2, -3), (4, 3, 4))
TO_SHORT = ((1, 4, 3), (1, 2, 1), (1, -3, -2), (2, 3, 1), (2, -2, -1), (3, 1, 0), (3, -1, 0))
FROM_SHORT = ((1, 0, 1), (1, 0, -1), (2, 1, 3), (2, 1, 2), (2, -1, -2), (3, 3, 4), (3, -2, -3))
TREES = ((TO_SHORT, FROM_RING, True), (TO_RING, FROM_RING, False))
WEIGHTS_AT = (((1,), (2,), (), (3,), (), ()), ((1,), (2,), (), (3,), (4,), ()))


def order(core):
    every, groups = range(NT), range(len(GROUPS))
    last_in, last_out = (tree[-1][0] for tree in TREES[core][:2])
    late = TREES[core][2]

    def weights(i):
        return [("weights", t, s) for s in WEIGHTS_AT[core][i] if s < last_out + (not late) for t in every]

    steps = [("near_weights", 1)]
    for s in range(1, last_in + 1):
        steps += [("reduce", t, s) for t in every] + [("near_weights", s + 1)] * (s < 4)
    steps += [("spread", i) for i in groups] + [("near_weights", 5)] + weights(0)
    steps += [("update", i) for i in groups] + weights(1)
    for i in groups:
        steps += [("near_updates", i)]
        for t in range(*GROUPS[i]):
            steps += [("updates", t, 1), ("squares", t)]
    steps += [("total", 0)] + weights(2)
    steps += [("updates", t, 2) for t in every] + weights(3) + [("total", 1), ("total", 2)]
    for s in range(3, last_out + (not late)):
        steps += [("updates", t, s) for t in every] + weights(s + 1)
    steps += [("total", 3)]
    if late:
        steps += [("late", t) for t in every]
    return steps + [("last", t) for t in every]


def side(t, h):
    return 1 if (t + h) % 2 == 0 else -1


def length(t, h, d):
    return 4 if (t + h + d) % 2 == 0 else 3


def kernel(
    g_hbm, w_hbm, m_hbm, v_hbm, lr_hbm, wd_hbm,
    all_w, all_u, scale_out, nf_out, ns_out, tr_out,
    g, w, m, v, nf, ns, lr, wd, ring, own, cross, u1, w1, passed, scale, sq_a, sq_b, sq_c, sq_x, squares,
    load_g, load_s, ring_s, ring_r, cross_s, cross_r, u1_s, u1_r, w1_s, w1_r, sq_s, sq_r, aw_s, aw_r, au_s, au_r, res_s, entered,
):
    dp, mp = lax.axis_index("dp"), lax.axis_index("mp")
    z, y = dp // SIDE, dp % SIDE

    def mod(i):
        return lax.rem(i + 2 * SIDE, SIDE)

    def ring_peer(h, k):
        return (z * SIDE + mod(y + k), mp) if h == 0 else (mod(z + k) * SIDE + y, mp)

    def cross_peer(h, k):
        return ring_peer(1 - h, k)

    def ring_at(h):
        return y if h == 0 else z

    def cross_at(h):
        return z if h == 0 else y

    def chunk(ref, t, h, r):
        return ref.at[t, 0, :, r] if h == 0 else ref.at[t, 1, r]

    def tile(ref, t, h, r, c):
        return ref.at[t, 0, c, r] if h == 0 else ref.at[t, 1, r, c]

    def send(src, dst, ss, rs, to):
        copy = pltpu.make_async_remote_copy(
            src_ref=src, dst_ref=dst, send_sem=ss, recv_sem=rs, device_id=to, device_id_type=MESH
        )
        copy.start()

    def arrived(ref, sem):
        pltpu.make_async_copy(ref, ref, sem).wait()

    small = [
        pltpu.make_async_copy(a, b, load_s.at[i])
        for i, (a, b) in enumerate(((w_hbm, w), (m_hbm, m), (v_hbm, v), (lr_hbm, lr), (wd_hbm, wd)))
    ]
    loads = [pltpu.make_async_copy(g_hbm.at[t, h], g.at[t, h], load_g.at[t, h]) for t in range(NT) for h in range(2)]
    for c in small + loads:
        c.start()

    other_core, along_x = (dp, mp + 1 - 2 * (mp % 2)), [(dp, mod(mp + k)) for k in (2, -2)]
    barrier = pltpu.get_barrier_semaphore()
    near = [ring_peer(h, k) for h in range(2) for k in (1, -1)]
    near += [other_core] + along_x
    for peer in near:
        pl.semaphore_signal(barrier, inc=1, device_id=peer, device_id_type=MESH)
    pl.semaphore_wait(barrier, len(near))
    for peer in along_x:
        pl.semaphore_signal(entered, inc=1, device_id=peer, device_id_type=MESH)

    first_fix = 1.0 - 0.9**STEP
    second_fix = 1.0 - 0.999**STEP
    def both_halves(core):
        held, seen = [], set()
        to_owner, from_owner, has_late = TREES[core]
        late_step = from_owner[-1][0] + (not has_late)

        def keep(src, dst, sem):
            held.append(pltpu.make_async_copy(src, dst, sem))
            held[-1].start()

        def block_sum(t, h, at, s):
            mine = chunk(g_hbm if s == 1 else g, t, h, mod(ring_at(h) - side(t, h) * at))
            parts = [ring.at[t, h, a % SIDE] for _, a, b in to_owner if b == at]
            for _, a, b in to_owner:
                if b == at:
                    arrived(ring.at[t, h, a % SIDE], ring_r.at[t, h, a % SIDE])
            return mine, parts

        def reduce(t, s):
            for h in range(2):
                if s == 2:
                    loads[2 * t + h].wait()
                for step, a, b in to_owner:
                    if step == s:
                        src, parts = block_sum(t, h, a, s)
                        if parts:
                            total = src[...]
                            for part in parts:
                                total += part[...]
                            src = parts[0]
                            src[...] = total
                        send(
                            src, ring.at[t, h, a % SIDE], ring_s, ring_r.at[t, h, a % SIDE],
                            ring_peer(h, side(t, h) * (b - a)),
                        )

        def near_weights(s):
            if s == 1:
                for c in small:
                    c.wait()
                for h in range(2):
                    w1[h, cross_at(h)] = w[:, h]
            for h in range(2):
                for d, sign in enumerate((1, -1)):
                    n = length(0, h, d)
                    if 1 < s <= n + 1:
                        at = w1.at[h, mod(cross_at(h) - sign * (s - 1))]
                        arrived(at, w1_r.at[h, d, s - 2])
                    if s <= n:
                        at = w1.at[h, mod(cross_at(h) - sign * (s - 1))]
                        send(at, at, w1_s, w1_r.at[h, d, s - 1], cross_peer(h, sign))

        def across(src, dst, i, ss, rs):
            lo, hi = GROUPS[i]
            for k in FAR_FIRST:
                for h in range(2):
                    at = cross_at(h) if src is u1 else mod(cross_at(h) + k)
                    send(src.at[h, at, lo:hi], dst.at[h, cross_at(h), lo:hi], ss, rs.at[i, h], cross_peer(h, k))

        def came_across(dst, i, rs):
            lo, hi = GROUPS[i]
            for h in range(2):
                arrived(dst.at[h, 0:7, lo:hi], rs.at[i, h])

        def spread(i):
            for t in range(*GROUPS[i]):
                for h in range(2):
                    src, parts = block_sum(t, h, 0, 5)
                    total = src[...]
                    for part in parts:
                        total += part[...]
                    own[h, :, t] = total
            across(own, cross, i, cross_s, cross_r)

        def update(i):
            lo, hi = GROUPS[i]
            for h in range(2):
                cross[h, cross_at(h), lo:hi] = own[h, cross_at(h), lo:hi]
            came_across(cross, i, cross_r)
            for h in range(2):
                summed = jnp.sum(cross[h, :, lo:hi], axis=0) * (1.0 / (SIDE * SIDE))
                new_first = 0.9 * m[lo:hi, h] + 0.1 * summed
                new_second = 0.999 * v[lo:hi, h] + 0.001 * summed * summed
                nf[lo:hi, h] = new_first
                ns[lo:hi, h] = new_second
                part = new_first / first_fix / (jnp.sqrt(new_second / second_fix) + 1e-06)
                for t in range(lo, hi):
                    u1[h, cross_at(h), t] = part[t - lo] + wd[t] * w[t, h]
            across(u1, u1, i, u1_s, u1_r)

        def squared(a):
            return jnp.sum(jnp.sum(a * a, axis=0), axis=0, keepdims=True)

        def near_updates(i):
            came_across(u1, i, u1_r)

        def squares_of(t):
            for h in range(2):
                squares[h, t : t + 1] = squared(w1[h, :, t])
                squares[h, NT + t : NT + t + 1] = squared(u1[h, :, t])

        def total(stage):
            if stage == 0:
                for h, slots in enumerate((sq_a, sq_b)):
                    slots[ring_at(h)] = squares[h]
                    for k in FAR_FIRST:
                        send(squares.at[h], slots.at[ring_at(h)], sq_s, sq_r.at[h], ring_peer(h, k))
            if stage == 1:
                for h, slots in enumerate((sq_a, sq_b)):
                    arrived(slots.at[0:7], sq_r.at[h])
                squares[2] = jnp.sum(sq_a[...], axis=0) + jnp.sum(sq_b[...], axis=0)
                sq_c[mp % 2] = squares[2]
                send(squares.at[2], sq_c.at[mp % 2], sq_s, sq_r.at[2], other_core)
            if stage == 2:
                arrived(sq_c.at[0], sq_r.at[2])
                squares[3] = sq_c[0] + sq_c[1]
                sq_x[mp // 2] = squares[3]
                pl.semaphore_wait(entered, 2)
                for k in (4, 2, 6):
                    send(squares.at[3], sq_x.at[mp // 2], sq_s, sq_r.at[3], (dp, mod(mp + k)))
            if stage == 3:
                arrived(sq_x.at[0:3], sq_r.at[3])
                both = jnp.sum(sq_x[...], axis=0)
                roots = jnp.sqrt(jnp.sum(both, axis=1, keepdims=True))
                ratio = roots[0:NT] / (roots[NT:] + 1e-06)
                for t in range(NT):
                    tr_out[t] = jnp.max(ratio[t : t + 1])
                    scale[t : t + 1] = jnp.broadcast_to(lr[t] * ratio[t : t + 1], (1, 128))
                keep(scale, scale_out, res_s.at[2])

        def around(first, ref, t, s, sems, sem):
            for h in range(2):
                for step, a, b in from_owner:
                    if step == s < late_step:
                        at = chunk(ref, t, h, place(t, h, a))
                        if a:
                            landed(ref, t, h, a, sems)
                        send(
                            at if a else first.at[h, :, t], at, sem, sems.at[t, h, b % SIDE],
                            ring_peer(h, side(t, h) * (b - a)),
                        )

        def place(t, h, a):
            return mod(ring_at(h) - side(t, h) * a)

        def landed(ref, t, h, a, sems):
            if (ref is all_w, t, h, a) not in seen:
                seen.add((ref is all_w, t, h, a))
                arrived(chunk(ref, t, h, place(t, h, a)), sems.at[t, h, a % SIDE])

        def late(t):
            for h in range(2):
                for step, a, b in from_owner:
                    if step == late_step:
                        landed(all_w, t, h, a, aw_r)
                        landed(all_u, t, h, a, au_r)
                        at = chunk(all_w, t, h, place(t, h, a))
                        new = passed.at[t, h, a % 2]
                        new[...] = at[...] - scale[t : t + 1] * chunk(all_u, t, h, place(t, h, a))[...]
                        send(new, at, aw_s, aw_r.at[t, h, b % SIDE], ring_peer(h, side(t, h) * (b - a)))

        def last(t):
            for h in range(2):
                for step, _, a in from_owner:
                    landed(all_w, t, h, a, aw_r)
                    if step < late_step:
                        landed(all_u, t, h, a, au_r)

        def weights(t, s):
            if s == 1:
                for h in range(2):
                    chunk(all_w, t, h, ring_at(h))[...] = w1[h, :, t]
                    for step, _, a in from_owner:
                        if step == late_step:
                            chunk(all_u, t, h, place(t, h, a))[...] = jnp.zeros((SIDE, 8, 128), F32)
            around(w1, all_w, t, s, aw_r, aw_s)

        def updates(t, s):
            around(u1, all_u, t, s, au_r, au_s)
            if s == 1:
                for h in range(2):
                    chunk(all_u, t, h, ring_at(h))[...] = u1[h, :, t]

        acts = {
            "reduce": reduce, "near_weights": near_weights, "spread": spread, "update": update,
            "near_updates": near_updates, "squares": squares_of, "total": total, "weights": weights, "updates": updates, "late": late, "last": last,
        }
        for name, *args in order(core):
            acts[name](*args)
            if name == "update" and args[0] == len(GROUPS) - 1:
                keep(nf, nf_out, res_s.at[0])
                keep(ns, ns_out, res_s.at[1])

        arrived(g.at[:, :, 0:7], ring_s)
        arrived(g.at[:, :, 0:7], aw_s)
        arrived(g.at[:, :, 0 : sum(step < late_step for step, _, _ in from_owner)], au_s)
        arrived(g.at[0, 0, 0:7], cross_s)
        arrived(g.at[0, 0, 0:7], u1_s)
        arrived(g.at[0, 0, 0:7], w1_s)
        arrived(g.at[0, 0:1, 0:3, 0:6], sq_s)
        for c in held:
            c.wait()

    for core in range(2):

        @pl.when(mp % 2 == core)
        def _(core=core):
            both_halves(core)


def results(all_w, all_u, scale, nf, ns, tr, new_out, nf_out, ns_out, tr_out, new, sem, sem_new):
    copies = [
        pltpu.make_async_copy(a, b, sem.at[i])
        for i, (a, b) in enumerate(((nf, nf_out), (ns, ns_out), (tr, tr_out)))
    ]
    for c in copies:
        c.start()
    for t in range(NT):
        for h in range(2):
            new[t, h] = all_w[t, h] - scale[t : t + 1] * all_u[t, h]
            copies.append(pltpu.make_async_copy(new.at[t, h], new_out.at[t, h], sem_new.at[t, h]))
            copies[-1].start()
    for c in copies:
        c.wait()


def shards(gradients, weights, first_moment, second_moment, learn_rate, weight_decay):
    tiles = (NT, 2, SIDE, SIDE, 8, 128)
    mine = (NT, 2, 8, 128)
    g = gradients.reshape(NT, 2, 8, SIDE, SIDE, 128).transpose(0, 1, 3, 4, 2, 5)
    dma = pltpu.SemaphoreType.DMA
    any_space = pl.BlockSpec(memory_space=pl.ANY)
    smem = pl.BlockSpec(memory_space=pltpu.SMEM)
    vmem = pl.BlockSpec(memory_space=pltpu.VMEM)
    arrays = pl.pallas_call(
        kernel,
        out_shape=(
            jax.ShapeDtypeStruct(tiles, F32),
            jax.ShapeDtypeStruct(tiles, F32),
            jax.ShapeDtypeStruct((8, 128), F32),
            jax.ShapeDtypeStruct(mine, F32),
            jax.ShapeDtypeStruct(mine, F32),
            jax.ShapeDtypeStruct((NT,), F32),
        ),
        in_specs=[any_space] * 6,
        out_specs=(vmem, vmem, *[any_space] * 3, smem),
        scratch_shapes=[
            pltpu.VMEM(tiles, F32),
            *[pltpu.VMEM(mine, F32)] * 5,
            *[pltpu.SMEM((NT,), F32)] * 2,
            pltpu.VMEM((NT, 2, SIDE, SIDE, 8, 128), F32),
            *[pltpu.VMEM((2, SIDE, NT, 8, 128), F32)] * 4,
            pltpu.VMEM((NT, 2, 2, SIDE, 8, 128), F32),
            pltpu.VMEM((8, 128), F32),
            *[pltpu.VMEM((SIDE, 8, 128), F32)] * 2,
            pltpu.VMEM((2, 8, 128), F32),
            pltpu.VMEM((4, 8, 128), F32),
            pltpu.VMEM((4, 8, 128), F32),
            dma((NT, 2)), dma((5,)),
            dma, dma((NT, 2, SIDE)),
            dma, dma((len(GROUPS), 2)),
            dma, dma((len(GROUPS), 2)),
            dma, dma((2, 2, 4)),
            dma, dma((4,)),
            dma, dma((NT, 2, SIDE)),
            dma, dma((NT, 2, SIDE)),
            dma((3,)),
            pltpu.SemaphoreType.REGULAR,
        ],
        compiler_params=pltpu.CompilerParams(
            collective_id=0, has_side_effects=True, vmem_limit_bytes=24 * 2**20
        ),
        name="lamb",
    )(
        *(
            pltpu.with_memory_space_constraint(a, pltpu.HBM)
            for a in (
                g, *(a.reshape(mine) for a in (weights, first_moment, second_moment)), learn_rate, weight_decay
            )
        )
    )
    out, nf, ns, tr = pl.pallas_call(
        results,
        out_shape=tuple(jax.ShapeDtypeStruct(a.shape, F32) for a in (arrays[0], *arrays[3:])),
        in_specs=[vmem] * 3 + [any_space] * 3,
        out_specs=(any_space,) * 4,
        scratch_shapes=[pltpu.VMEM(tiles, F32), dma((3,)), dma((NT, 2))],
        compiler_params=pltpu.CompilerParams(vmem_limit_bytes=8 * 2**20),
        name="results",
    )(*(pltpu.with_memory_space_constraint(a, pltpu.VMEM) for a in arrays))
    new_weights = out.transpose(0, 1, 4, 2, 3, 5).reshape(NT, 16, SIDE * SIDE * 128)
    return new_weights, nf.reshape(NT, 16, 128), ns.reshape(NT, 16, 128), tr


def solution(mesh):
    in_specs = (
        P("dp", None, "mp", None),
        P(None, "mp", "dp"),
        P(None, "mp", "dp"),
        P(None, "mp", "dp"),
        P(),
        P(),
    )
    out_specs = (P(None, "mp", None), P(None, "mp", "dp"), P(None, "mp", "dp"), P())
    return jax.shard_map(shards, mesh=mesh, in_specs=in_specs, out_specs=out_specs, check_vma=False)
```

```python
import functools

import jax
import jax.numpy as jnp
from jax import lax
from jax.experimental import pallas as pl
from jax.experimental.pallas import tpu as pltpu
from jax.sharding import PartitionSpec as P

STEP = 10
GROUPS = ((0, 1), (1, 2), (2, 3), (3, 4))
FAR_FIRST = (4, 3, 5, 2, 6, 1, 7)
NT = 4
SIDE = 8
F32 = jnp.float32
MESH = pl.DeviceIdType.MESH


TO_RING = ((1, 4, 3), (1, -3, -2), (2, 3, 2), (2, -2, -1), (3, 2, 1), (3, -1, 0), (4, 1, 0))
FROM_RING = ((1, 0, 1), (1, 0, -1), (2, 1, 2), (2, -1, -2), (3, 2, 3), (3, -2, -3), (4, 3, 4))
TO_SHORT = ((1, 4, 3), (1, 2, 1), (1, -3, -2), (2, 3, 1), (2, -2, -1), (3, 1, 0), (3, -1, 0))
FROM_SHORT = ((1, 0, 1), (1, 0, -1), (2, 1, 3), (2, 1, 2), (2, -1, -2), (3, 3, 4), (3, -2, -3))
TREES = ((TO_SHORT, FROM_RING, True), (TO_RING, FROM_RING, False))
WEIGHTS_AT = (((1,), (2,), (), (3,), (), ()), ((1,), (2,), (), (3,), (4,), ()))


def order(core):
    every, groups = range(NT), range(len(GROUPS))
    last_in, last_out = (tree[-1][0] for tree in TREES[core][:2])
    late = TREES[core][2]

    def weights(i):
        return [("weights", t, s) for s in WEIGHTS_AT[core][i] if s < last_out + (not late) for t in every]

    steps = [("near_weights", 1)]
    for s in range(1, last_in + 1):
        steps += [("reduce", t, s) for t in every] + [("near_weights", s + 1)] * (s < 4)
    steps += [("spread", i) for i in groups] + [("near_weights", 5)] + weights(0)
    steps += [("update", i) for i in groups] + weights(1)
    for i in groups:
        steps += [("near_updates", i)]
        for t in range(*GROUPS[i]):
            steps += [("updates", t, 1), ("squares", t)]
    steps += [("total", 0)] + weights(2)
    steps += [("updates", t, 2) for t in every] + weights(3) + [("total", 1), ("total", 2)]
    for s in range(3, last_out + (not late)):
        steps += [("updates", t, s) for t in every] + weights(s + 1)
    steps += [("total", 3)]
    if late:
        steps += [("late", t) for t in every]
    return steps + [("last", t) for t in every]


def side(t, h):
    return 1 if (t + h) % 2 == 0 else -1


def length(t, h, d):
    return 4 if (t + h + d) % 2 == 0 else 3


def kernel(
    g_hbm, w_hbm, m_hbm, v_hbm, lr_hbm, wd_hbm,
    all_w, all_u, scale_out, nf_out, ns_out, tr_out,
    g, w, m, v, nf, ns, lr, wd, ring, own, cross, u1, w1, passed, scale, sq_a, sq_b, sq_c, sq_x, squares,
    load_g, load_s, ring_s, ring_r, cross_s, cross_r, u1_s, u1_r, w1_s, w1_r, sq_s, sq_r, aw_s, aw_r, au_s, au_r, res_s, entered,
):
    dp, mp = lax.axis_index("dp"), lax.axis_index("mp")
    z, y = dp // SIDE, dp % SIDE

    def mod(i):
        return lax.rem(i + 2 * SIDE, SIDE)

    def ring_peer(h, k):
        return (z * SIDE + mod(y + k), mp) if h == 0 else (mod(z + k) * SIDE + y, mp)

    def cross_peer(h, k):
        return ring_peer(1 - h, k)

    def ring_at(h):
        return y if h == 0 else z

    def cross_at(h):
        return z if h == 0 else y

    def chunk(ref, t, h, r):
        return ref.at[t, 0, :, r] if h == 0 else ref.at[t, 1, r]

    def tile(ref, t, h, r, c):
        return ref.at[t, 0, c, r] if h == 0 else ref.at[t, 1, r, c]

    def send(src, dst, ss, rs, to):
        copy = pltpu.make_async_remote_copy(
            src_ref=src, dst_ref=dst, send_sem=ss, recv_sem=rs, device_id=to, device_id_type=MESH
        )
        copy.start()

    def arrived(ref, sem):
        pltpu.make_async_copy(ref, ref, sem).wait()

    small = [
        pltpu.make_async_copy(a, b, load_s.at[i])
        for i, (a, b) in enumerate(((w_hbm, w), (m_hbm, m), (v_hbm, v), (lr_hbm, lr), (wd_hbm, wd)))
    ]
    loads = [pltpu.make_async_copy(g_hbm.at[t, h], g.at[t, h], load_g.at[t, h]) for t in range(NT) for h in range(2)]
    for c in small[:1] + loads + small[1:]:
        c.start()

    other_core, along_x = (dp, mp + 1 - 2 * (mp % 2)), [(dp, mod(mp + k)) for k in (2, -2)]
    barrier = pltpu.get_barrier_semaphore()
    near = [ring_peer(h, k) for h in range(2) for k in (1, -1)]
    near += [other_core] + along_x
    for peer in near:
        pl.semaphore_signal(barrier, inc=1, device_id=peer, device_id_type=MESH)
    pl.semaphore_wait(barrier, len(near))
    for peer in along_x:
        pl.semaphore_signal(entered, inc=1, device_id=peer, device_id_type=MESH)

    first_fix = 1.0 - 0.9**STEP
    second_fix = 1.0 - 0.999**STEP
    def both_halves(core):
        held, seen = [], set()
        to_owner, from_owner, has_late = TREES[core]
        late_step = from_owner[-1][0] + (not has_late)

        def keep(src, dst, sem):
            held.append(pltpu.make_async_copy(src, dst, sem))
            held[-1].start()

        def block_sum(t, h, at, s):
            mine = chunk(g, t, h, mod(ring_at(h) - side(t, h) * at))
            parts = [ring.at[t, h, a % SIDE] for _, a, b in to_owner if b == at]
            for _, a, b in to_owner:
                if b == at:
                    arrived(ring.at[t, h, a % SIDE], ring_r.at[t, h, a % SIDE])
            return mine, parts

        def reduce(t, s):
            for h in range(2):
                if s == 1:
                    loads[2 * t + h].wait()
                for step, a, b in to_owner:
                    if step == s:
                        src, parts = block_sum(t, h, a, s)
                        if parts:
                            total = src[...]
                            for part in parts:
                                total += part[...]
                            src = parts[0]
                            src[...] = total
                        send(
                            src, ring.at[t, h, a % SIDE], ring_s, ring_r.at[t, h, a % SIDE],
                            ring_peer(h, side(t, h) * (b - a)),
                        )

        def near_weights(s):
            if s == 1:
                for c in small:
                    c.wait()
                for h in range(2):
                    w1[h, cross_at(h)] = w[:, h]
            for h in range(2):
                for d, sign in enumerate((1, -1)):
                    n = length(0, h, d)
                    if 1 < s <= n + 1:
                        at = w1.at[h, mod(cross_at(h) - sign * (s - 1))]
                        arrived(at, w1_r.at[h, d, s - 2])
                    if s <= n:
                        at = w1.at[h, mod(cross_at(h) - sign * (s - 1))]
                        send(at, at, w1_s, w1_r.at[h, d, s - 1], cross_peer(h, sign))

        def across(src, dst, i, ss, rs):
            lo, hi = GROUPS[i]
            for k in FAR_FIRST:
                for h in range(2):
                    at = cross_at(h) if src is u1 else mod(cross_at(h) + k)
                    send(src.at[h, at, lo:hi], dst.at[h, cross_at(h), lo:hi], ss, rs.at[i, h], cross_peer(h, k))

        def came_across(dst, i, rs):
            lo, hi = GROUPS[i]
            for h in range(2):
                arrived(dst.at[h, 0:7, lo:hi], rs.at[i, h])

        def spread(i):
            for t in range(*GROUPS[i]):
                for h in range(2):
                    src, parts = block_sum(t, h, 0, 5)
                    total = src[...]
                    for part in parts:
                        total += part[...]
                    own[h, :, t] = total
            across(own, cross, i, cross_s, cross_r)

        def update(i):
            lo, hi = GROUPS[i]
            for h in range(2):
                cross[h, cross_at(h), lo:hi] = own[h, cross_at(h), lo:hi]
            came_across(cross, i, cross_r)
            for h in range(2):
                summed = jnp.sum(cross[h, :, lo:hi], axis=0) * (1.0 / (SIDE * SIDE))
                new_first = 0.9 * m[lo:hi, h] + 0.1 * summed
                new_second = 0.999 * v[lo:hi, h] + 0.001 * summed * summed
                nf[lo:hi, h] = new_first
                ns[lo:hi, h] = new_second
                part = new_first / first_fix / (jnp.sqrt(new_second / second_fix) + 1e-06)
                for t in range(lo, hi):
                    u1[h, cross_at(h), t] = part[t - lo] + wd[t] * w[t, h]
            across(u1, u1, i, u1_s, u1_r)

        def squared(a):
            return jnp.sum(jnp.sum(a * a, axis=0), axis=0, keepdims=True)

        def near_updates(i):
            came_across(u1, i, u1_r)

        def squares_of(t):
            for h in range(2):
                squares[h, t : t + 1] = squared(w1[h, :, t])
                squares[h, NT + t : NT + t + 1] = squared(u1[h, :, t])

        def total(stage):
            if stage == 0:
                for h, slots in enumerate((sq_a, sq_b)):
                    slots[ring_at(h)] = squares[h]
                    for k in FAR_FIRST:
                        send(squares.at[h], slots.at[ring_at(h)], sq_s, sq_r.at[h], ring_peer(h, k))
            if stage == 1:
                for h, slots in enumerate((sq_a, sq_b)):
                    arrived(slots.at[0:7], sq_r.at[h])
                squares[2] = jnp.sum(sq_a[...], axis=0) + jnp.sum(sq_b[...], axis=0)
                sq_c[mp % 2] = squares[2]
                send(squares.at[2], sq_c.at[mp % 2], sq_s, sq_r.at[2], other_core)
            if stage == 2:
                arrived(sq_c.at[0], sq_r.at[2])
                squares[3] = sq_c[0] + sq_c[1]
                sq_x[mp // 2] = squares[3]
                pl.semaphore_wait(entered, 2)
                for k in (4, 2, 6):
                    send(squares.at[3], sq_x.at[mp // 2], sq_s, sq_r.at[3], (dp, mod(mp + k)))
            if stage == 3:
                arrived(sq_x.at[0:3], sq_r.at[3])
                both = jnp.sum(sq_x[...], axis=0)
                roots = jnp.sqrt(jnp.sum(both, axis=1, keepdims=True))
                ratio = roots[0:NT] / (roots[NT:] + 1e-06)
                for t in range(NT):
                    tr_out[t] = jnp.max(ratio[t : t + 1])
                    scale[t : t + 1] = jnp.broadcast_to(lr[t] * ratio[t : t + 1], (1, 128))
                keep(scale, scale_out, res_s.at[2])

        def around(first, ref, t, s, sems, sem):
            for h in range(2):
                for step, a, b in from_owner:
                    if step == s < late_step:
                        at = chunk(ref, t, h, place(t, h, a))
                        if a:
                            landed(ref, t, h, a, sems)
                        send(
                            at if a else first.at[h, :, t], at, sem, sems.at[t, h, b % SIDE],
                            ring_peer(h, side(t, h) * (b - a)),
                        )

        def place(t, h, a):
            return mod(ring_at(h) - side(t, h) * a)

        def landed(ref, t, h, a, sems):
            if (ref is all_w, t, h, a) not in seen:
                seen.add((ref is all_w, t, h, a))
                arrived(chunk(ref, t, h, place(t, h, a)), sems.at[t, h, a % SIDE])

        def late(t):
            for h in range(2):
                for step, a, b in from_owner:
                    if step == late_step:
                        landed(all_w, t, h, a, aw_r)
                        landed(all_u, t, h, a, au_r)
                        at = chunk(all_w, t, h, place(t, h, a))
                        new = passed.at[t, h, a % 2]
                        new[...] = at[...] - scale[t : t + 1] * chunk(all_u, t, h, place(t, h, a))[...]
                        send(new, at, aw_s, aw_r.at[t, h, b % SIDE], ring_peer(h, side(t, h) * (b - a)))

        def last(t):
            for h in range(2):
                for step, _, a in from_owner:
                    landed(all_w, t, h, a, aw_r)
                    if step < late_step:
                        landed(all_u, t, h, a, au_r)

        def weights(t, s):
            if s == 1:
                for h in range(2):
                    chunk(all_w, t, h, ring_at(h))[...] = w1[h, :, t]
                    for step, _, a in from_owner:
                        if step == late_step:
                            chunk(all_u, t, h, place(t, h, a))[...] = jnp.zeros((SIDE, 8, 128), F32)
            around(w1, all_w, t, s, aw_r, aw_s)

        def updates(t, s):
            around(u1, all_u, t, s, au_r, au_s)
            if s == 1:
                for h in range(2):
                    chunk(all_u, t, h, ring_at(h))[...] = u1[h, :, t]

        acts = {
            "reduce": reduce, "near_weights": near_weights, "spread": spread, "update": update,
            "near_updates": near_updates, "squares": squares_of, "total": total, "weights": weights, "updates": updates, "late": late, "last": last,
        }
        for name, *args in order(core):
            acts[name](*args)
            if name == "update" and args[0] == len(GROUPS) - 1:
                keep(nf, nf_out, res_s.at[0])
                keep(ns, ns_out, res_s.at[1])

        arrived(g.at[:, :, 0:7], ring_s)
        arrived(g.at[:, :, 0:7], aw_s)
        arrived(g.at[:, :, 0 : sum(step < late_step for step, _, _ in from_owner)], au_s)
        arrived(g.at[0, 0, 0:7], cross_s)
        arrived(g.at[0, 0, 0:7], u1_s)
        arrived(g.at[0, 0, 0:7], w1_s)
        arrived(g.at[0, 0:1, 0:3, 0:6], sq_s)
        for c in held:
            c.wait()

    for core in range(2):

        @pl.when(mp % 2 == core)
        def _(core=core):
            both_halves(core)


def results(all_w, all_u, scale, nf, ns, tr, new_out, nf_out, ns_out, tr_out, new, sem, sem_new):
    copies = [
        pltpu.make_async_copy(a, b, sem.at[i])
        for i, (a, b) in enumerate(((nf, nf_out), (ns, ns_out), (tr, tr_out)))
    ]
    for c in copies:
        c.start()
    for t in range(NT):
        for h in range(2):
            new[t, h] = all_w[t, h] - scale[t : t + 1] * all_u[t, h]
            copies.append(pltpu.make_async_copy(new.at[t, h], new_out.at[t, h], sem_new.at[t, h]))
            copies[-1].start()
    for c in copies:
        c.wait()


def shards(gradients, weights, first_moment, second_moment, learn_rate, weight_decay):
    tiles = (NT, 2, SIDE, SIDE, 8, 128)
    mine = (NT, 2, 8, 128)
    g = gradients.reshape(NT, 2, 8, SIDE, SIDE, 128).transpose(0, 1, 3, 4, 2, 5)
    dma = pltpu.SemaphoreType.DMA
    any_space = pl.BlockSpec(memory_space=pl.ANY)
    smem = pl.BlockSpec(memory_space=pltpu.SMEM)
    vmem = pl.BlockSpec(memory_space=pltpu.VMEM)
    arrays = pl.pallas_call(
        kernel,
        out_shape=(
            jax.ShapeDtypeStruct(tiles, F32),
            jax.ShapeDtypeStruct(tiles, F32),
            jax.ShapeDtypeStruct((8, 128), F32),
            jax.ShapeDtypeStruct(mine, F32),
            jax.ShapeDtypeStruct(mine, F32),
            jax.ShapeDtypeStruct((NT,), F32),
        ),
        in_specs=[any_space] * 6,
        out_specs=(vmem, vmem, *[any_space] * 3, smem),
        scratch_shapes=[
            pltpu.VMEM(tiles, F32),
            *[pltpu.VMEM(mine, F32)] * 5,
            *[pltpu.SMEM((NT,), F32)] * 2,
            pltpu.VMEM((NT, 2, SIDE, SIDE, 8, 128), F32),
            *[pltpu.VMEM((2, SIDE, NT, 8, 128), F32)] * 4,
            pltpu.VMEM((NT, 2, 2, SIDE, 8, 128), F32),
            pltpu.VMEM((8, 128), F32),
            *[pltpu.VMEM((SIDE, 8, 128), F32)] * 2,
            pltpu.VMEM((2, 8, 128), F32),
            pltpu.VMEM((4, 8, 128), F32),
            pltpu.VMEM((4, 8, 128), F32),
            dma((NT, 2)), dma((5,)),
            dma, dma((NT, 2, SIDE)),
            dma, dma((len(GROUPS), 2)),
            dma, dma((len(GROUPS), 2)),
            dma, dma((2, 2, 4)),
            dma, dma((4,)),
            dma, dma((NT, 2, SIDE)),
            dma, dma((NT, 2, SIDE)),
            dma((3,)),
            pltpu.SemaphoreType.REGULAR,
        ],
        compiler_params=pltpu.CompilerParams(
            collective_id=0, has_side_effects=True, vmem_limit_bytes=24 * 2**20
        ),
        name="lamb",
    )(
        *(
            pltpu.with_memory_space_constraint(a, pltpu.HBM)
            for a in (
                g, *(a.reshape(mine) for a in (weights, first_moment, second_moment)), learn_rate, weight_decay
            )
        )
    )
    out, nf, ns, tr = pl.pallas_call(
        results,
        out_shape=tuple(jax.ShapeDtypeStruct(a.shape, F32) for a in (arrays[0], *arrays[3:])),
        in_specs=[vmem] * 3 + [any_space] * 3,
        out_specs=(any_space,) * 4,
        scratch_shapes=[pltpu.VMEM(tiles, F32), dma((3,)), dma((NT, 2))],
        compiler_params=pltpu.CompilerParams(vmem_limit_bytes=8 * 2**20),
        name="results",
    )(*(pltpu.with_memory_space_constraint(a, pltpu.VMEM) for a in arrays))
    new_weights = out.transpose(0, 1, 4, 2, 3, 5).reshape(NT, 16, SIDE * SIDE * 128)
    return new_weights, nf.reshape(NT, 16, 128), ns.reshape(NT, 16, 128), tr


def solution(mesh):
    in_specs = (
        P("dp", None, "mp", None),
        P(None, "mp", "dp"),
        P(None, "mp", "dp"),
        P(None, "mp", "dp"),
        P(),
        P(),
    )
    out_specs = (P(None, "mp", None), P(None, "mp", "dp"), P(None, "mp", "dp"), P())
    return jax.shard_map(shards, mesh=mesh, in_specs=in_specs, out_specs=out_specs, check_vma=False)
```
